256 devices in a mesh: tm: 4 (over z_lo, core), space: 64 (over x, y, z_hi).
Axes of the slice: x: 4, y: 4, z: 8 (z_hi: 4, z_lo: 2; z = z_hi * 2 + z_lo), core: 2. Of those that a mesh axis runs over, the one named last changes fastest.
Arguments:
- trajectory: float32 [8, 4, 512, 512], P('tm', None, 'space'), may hold values from -6 to 6
- noise: float32 [8, 4, 512, 512], P('tm', None, 'space'), may hold values from -6 to 6
- step_size: float32 [8], P('tm'), may hold values from 0.2 to 0.6
- noise_scale: float32 [8], P('tm'), may hold values from 0.2 to 0.5
- time_bias: float32 [8, 128], P('tm'), may hold values from -5 to 5
- start_state: float32 [4, 512, 512], P(None, 'space'), may hold values from -6 to 6
- observed: float32 [4, 512, 512], P(None, 'space'), may hold values from -6 to 6
- conv_in: bfloat16 [9, 128, 4], replicated, may hold values from -1 to 1
- conv_mid: bfloat16 [9, 128, 128], replicated, may hold values from -0.1875 to 0.1875
- conv_out: bfloat16 [9, 4, 128], replicated, may hold values from -0.1875 to 0.1875
- psf_bank: float32 [16, 4, 25], replicated, may hold values from 0.02 to 0.12
- index_map: int32 [64, 64], replicated, may hold values from 0 to 15
Outputs:
- new_trajectory: float32 [8, 4, 512, 512], P('tm', None, 'space')
The draws below stay inside these ranges and needn't reach their ends.
All inputs are finite; a program needn't handle non-finite values.
Results may differ from the reference program's by a relative error of at most 0.0024.
Values may be sent and summed in bfloat16 or wider, within the bound.
No kernel may reach another device: no remote copies, remote signals or barrier semaphores. Data moves between devices by JAX's collectives and lax.ppermute only.
A program may use at most 128 MiB of HBM per device.

```python
import math
import jax
import jax.numpy as jnp

BANDS = 4
C = 128
NPSF = 16
TAPS = 25
BLOCK = 8
W = 512
TSTEPS = 8
H = 512


def plant(entries, stream_key, low, largest):
    longest = entries.shape.index(max(entries.shape))
    spots = []
    for shift in (0, 1):
        where = [jax.random.randint(jax.random.fold_in(stream_key, axis), (), 0, length) for axis, length in enumerate(entries.shape)]
        where[longest] = (where[longest] + shift) % entries.shape[longest]
        spots.append(tuple(where))
    return entries.at[spots[0]].set(low).at[spots[1]].set(largest)


def block_levels(rng, extent, shards, smallest, high):
    gain, own = 1.0, jax.random.fold_in(rng, 6)
    for dim, blocks in shards:
        draws = jnp.exp(jax.random.uniform(jax.random.fold_in(own, dim), (blocks,), jnp.float32, smallest / len(shards), high / len(shards)))
        gain = gain * jnp.repeat(draws, extent[dim] // blocks).reshape([-1 if axis == dim else 1 for axis in range(len(extent))])
    return gain


def centred(rng, shape, scale, bound, pieces=(), held_as=jnp.bfloat16):
    values = scale * jax.random.normal(rng, shape, jnp.float32)
    if pieces:
        values = values * block_levels(rng, shape, pieces, -0.22, 0.18)
    return jnp.clip(values, -bound, bound).astype(held_as)


def setup_inputs(seed: int = 0) -> dict:
    keys = jax.random.split(jax.random.key(seed), 13)
    return {
        "trajectory": centred(keys[0], (TSTEPS, BANDS, H, W), 1.0, 6.0, ((0, 4), (2, 64)), jnp.float32),
        "noise": centred(keys[1], (TSTEPS, BANDS, H, W), 1.0, 6.0, ((0, 4), (2, 64)), jnp.float32),
        "step_size": jnp.clip(jnp.exp(math.log(0.6) - 1.0986123 * jax.random.uniform(keys[2], (TSTEPS,), jnp.float32) ** block_levels(keys[2], (TSTEPS,), ((0, 4),), -0.2, 0.2)), 0.2, 0.6),
        "noise_scale": jnp.clip(jnp.exp(math.log(0.5) - 0.9162907 * jax.random.uniform(keys[3], (TSTEPS,), jnp.float32) ** block_levels(keys[3], (TSTEPS,), ((0, 4),), -0.2, 0.2)), 0.2, 0.5),
        "time_bias": centred(keys[4], (TSTEPS, C), 1.0, 5.0, ((0, 4),), jnp.float32),
        "start_state": centred(keys[5], (BANDS, H, W), 1.0, 6.0, ((1, 64),), jnp.float32),
        "observed": centred(keys[6], (BANDS, H, W), 1.0, 6.0, ((1, 64),), jnp.float32),
        "conv_in": centred(keys[7], (9, C, BANDS), (9 * BANDS) ** -0.5, 1.0),
        "conv_mid": centred(keys[8], (9, C, C), (9 * C) ** -0.5, 0.1875),
        "conv_out": centred(keys[9], (9, BANDS, C), (9 * C) ** -0.5, 0.1875),
        "psf_bank": jnp.clip(jnp.exp(jax.random.uniform(keys[10], (NPSF, BANDS, TAPS), jnp.float32, math.log(0.02), math.log(0.12))), 0.02, 0.12),
        "index_map": plant(jax.random.randint(keys[11], (H // BLOCK, W // BLOCK), 0, NPSF), jax.random.fold_in(keys[11], 1), 0, NPSF - 1).astype(jnp.int32),
    }


def conv_same(source, kernel):
    chans, height, width = source.shape
    padded = jnp.pad(source, ((0, 0), (1, 1), (1, 1)))
    total = jnp.zeros((kernel.shape[1], height * width), jnp.float32)
    for tap in range(9):
        row_off = tap // 3
        col_off = tap % 3
        window = padded[:, row_off:row_off + height, col_off:col_off + width].reshape(chans, height * width)
        total = total + jnp.dot(kernel[tap], window, preferred_element_type=jnp.float32)
    return total.reshape(kernel.shape[1], height, width)


def pixel_weights(psf_bank, index_map):
    pixel_index = jnp.repeat(jnp.repeat(index_map, BLOCK, axis=0), BLOCK, axis=1).astype(jnp.int32)
    picked = jnp.take(psf_bank, pixel_index, axis=0)
    return jnp.transpose(picked, (2, 3, 0, 1))


def blur_forward(field, weights):
    height, width = field.shape[1], field.shape[2]
    padded = jnp.pad(field, ((0, 0), (2, 2), (2, 2)))
    total = jnp.zeros(field.shape, jnp.float32)
    for tap in range(25):
        row_off = tap // 5
        col_off = tap % 5
        total = total + weights[:, tap] * padded[:, row_off:row_off + height, col_off:col_off + width]
    return total


def blur_adjoint(misfit, weights):
    height, width = misfit.shape[1], misfit.shape[2]
    total = jnp.zeros(misfit.shape, jnp.float32)
    for tap in range(25):
        row_off = tap // 5
        col_off = tap % 5
        padded = jnp.pad(weights[:, tap] * misfit, ((0, 0), (2, 2), (2, 2)))
        total = total + padded[:, 4 - row_off:4 - row_off + height, 4 - col_off:4 - col_off + width]
    return total


def reference(trajectory, noise, step_size, noise_scale, time_bias, start_state, observed, conv_in, conv_mid, conv_out, psf_bank, index_map):
    weights = pixel_weights(psf_bank, index_map)
    running = jnp.zeros(start_state.shape, jnp.float32)
    results = []
    for moment in range(TSTEPS):
        state = trajectory[moment]
        hidden_one = jax.nn.silu(conv_same(state.astype(jnp.bfloat16), conv_in) + time_bias[moment][:, None, None]).astype(jnp.bfloat16)
        hidden_two = (hidden_one.astype(jnp.float32) + jax.nn.silu(conv_same(hidden_one, conv_mid))).astype(jnp.bfloat16)
        score = conv_same(hidden_two, conv_out)
        guidance = blur_adjoint(observed - blur_forward(state, weights), weights)
        drift = step_size[moment] * (score + guidance) + noise_scale[moment] * noise[moment]
        running = running + drift
        results.append(start_state + running)
    return jnp.stack(results, axis=0)
```

```python
import jax
import jax.numpy as jnp
from jax import lax
from jax.experimental import pallas as pl
from jax.experimental.pallas import tpu as pltpu
from jax.sharding import PartitionSpec as P

F32 = jnp.float32
BF16 = jnp.bfloat16
B = 4
R = 8
W = 512
C = 128
TH = 2
HALO = 4
OH = 2
PACK = TH * B * HALO + B * OH
GRP = 16
STR = W // GRP
NPSF = 16
NT = (((1,), (1,)), ((), ()))


def dot(a, b):
    return jnp.dot(a, b, preferred_element_type=F32)


def dot_nt(a, b):
    return lax.dot_general(a, b, NT, preferred_element_type=F32)


def silu(v):
    half = 0.5 * v
    return half + half * jnp.tanh(half)


def shifted(v, by):
    if by == 0:
        return v
    lane = lax.broadcasted_iota(jnp.int32, v.shape, v.ndim - 1)
    moved = pltpu.roll(v, (-by) % W, v.ndim - 1)
    inside = lane < W - by if by > 0 else lane >= -by
    return jnp.where(inside, moved, 0.0)


def pack_kernel(x_ref, obs_ref, a_ref, b_ref, head, tail):
    odd = lax.rem(lax.axis_index("space"), 2) == 1
    for t in range(TH):
        for b in range(B):
            at = (t * B + b) * HALO
            head[at : at + HALO] = x_ref[t, b, :HALO]
            tail[at : at + HALO] = x_ref[t, b, R - HALO :]
    for b in range(B):
        at = TH * B * HALO + b * OH
        head[at : at + OH] = obs_ref[b, :OH]
        tail[at : at + OH] = obs_ref[b, R - OH :]
    first, last = head[...], tail[...]
    a_ref[...] = jnp.where(odd, first, last).astype(BF16)
    b_ref[...] = jnp.where(odd, last, first).astype(BF16)


def main_kernel(
    x_ref, noise_ref, step_ref, scale_ref, bias_ref, start_ref, obs_ref,
    a_ref, b_ref, win_ref, wmid_ref, wout_ref, psf_ref, map_ref,
    loc_ref, tot_ref,
    xs, xcol, obs, mis, wts, perm, h1, h2, halo,
):
    place = lax.axis_index("space")
    top = place == 0
    bottom = place == lax.axis_size("space") - 1
    odd = lax.rem(place, 2) == 1

    q = lax.broadcasted_iota(jnp.int32, (W, W), 0)
    c = lax.broadcasted_iota(jnp.int32, (W, W), 1)
    perm[...] = jnp.where((q & (GRP - 1)) * STR + (q >> 4) == c, 1.0, 0.0).astype(BF16)

    count = map_ref.shape[0]
    spread = jnp.where(
        lax.broadcasted_iota(jnp.int32, (count, W), 1) // R
        == lax.broadcasted_iota(jnp.int32, (count, W), 0),
        1.0,
        0.0,
    ).astype(BF16)
    psf = psf_ref[...]
    psf_hi = psf.astype(BF16)
    rest = psf - psf_hi.astype(F32)
    psf_mid = rest.astype(BF16)
    psf_lo = (rest - psf_mid.astype(F32)).astype(BF16)
    for n in range(3):
        row = jnp.clip(place + (n - 1), 0, count - 1)
        index = map_ref[pl.ds(row, 1), :].astype(F32).astype(BF16)
        pixel = dot(jnp.broadcast_to(index, (16, count)), spread)
        kind = lax.broadcasted_iota(jnp.int32, (NPSF, W), 0).astype(F32)
        one_hot = jnp.where(pixel[:NPSF] == kind, 1.0, 0.0).astype(BF16)
        wts[n] = dot(psf_hi, one_hot) + dot(psf_mid, one_hot) + dot(psf_lo, one_hot)

    got_a, got_b = a_ref[...].astype(F32), b_ref[...].astype(F32)
    halo[0] = jnp.where(top, 0.0, jnp.where(odd, got_a, got_b))
    halo[1] = jnp.where(bottom, 0.0, jnp.where(odd, got_b, got_a))
    for k in range(TH * B):
        xs[k, 0:HALO] = halo[0, k * HALO : (k + 1) * HALO]
        xs[k, HALO : HALO + R] = x_ref[k // B, k % B]
        xs[k, HALO + R : 2 * HALO + R] = halo[1, k * HALO : (k + 1) * HALO]
        xs[k, 2 * HALO + R :] = jnp.zeros((8, W), F32)
    for b in range(B):
        at = TH * B * HALO + b * OH
        obs[b, 0:OH] = halo[0, at : at + OH]
        obs[b, OH : OH + R] = obs_ref[b]
        obs[b, OH + R : 2 * OH + R] = halo[1, at : at + OH]
        obs[b, 2 * OH + R :] = jnp.zeros((4, W), F32)

    for n, by in enumerate((-2, -1, 0, 1, 2)):
        for k in range(TH * B):
            xcol[n, k] = shifted(xs[k], by)
    sub = lax.broadcasted_iota(jnp.int32, (R, W), 0)
    keep_one = jnp.logical_or(sub >= OH, jnp.logical_not(top))
    keep_two = jnp.logical_or(sub < OH, jnp.logical_not(bottom))
    guidance = [None] * (TH * B)
    for b in range(B):
        one = [jnp.zeros((R, W), F32) for _ in range(TH)]
        two = [jnp.zeros((R, W), F32) for _ in range(TH)]
        for tap in range(25):
            i = tap // 5
            up, own, down = (wts[n, pl.ds(b * 25 + tap, 1), :] for n in range(3))
            w_one = jnp.where(sub < OH, up, own)
            w_two = jnp.where(sub < OH, own, down)
            for t in range(TH):
                one[t] = one[t] + w_one * xcol[tap % 5, t * B + b, i : i + R]
                two[t] = two[t] + w_two * xcol[tap % 5, t * B + b, R + i : 2 * R + i]
        for t in range(TH):
            mis[t * B + b, :R] = jnp.where(keep_one, obs[b, :R] - one[t], 0.0)
            mis[t * B + b, R:] = jnp.where(keep_two, obs[b, R:] - two[t], 0.0)
        total = [jnp.zeros((R, W), F32) for _ in range(TH)]
        for j in range(5):
            part = [jnp.zeros((R, W), F32) for _ in range(TH)]
            for i in range(5):
                off = i - 2
                up, own, down = (wts[n, pl.ds(b * 25 + i * 5 + j, 1), :] for n in range(3))
                if off > 0:
                    w = jnp.where(sub < off, up, own)
                elif off < 0:
                    w = jnp.where(sub >= R + off, down, own)
                else:
                    w = own
                for t in range(TH):
                    part[t] = part[t] + w * mis[t * B + b, OH - off : OH - off + R]
            for t in range(TH):
                total[t] = total[t] + shifted(part[t], 2 - j)
        for t in range(TH):
            guidance[t * B + b] = total[t]

    running = [None] * B
    for t in range(TH):
        flat = xs[t * B : (t + 1) * B, : 2 * R].reshape(B * 2 * R, W)
        taps = jnp.concatenate([shifted(flat, by) for by in (-1, 0, 1)], axis=0).astype(BF16)
        source = dot_nt(perm[...], taps).astype(BF16)
        bias = bias_ref[t : t + 1, :]
        bias = jnp.concatenate([bias, bias], axis=1)
        edge_row = lax.broadcasted_iota(jnp.int32, (GRP, 2 * C), 0)
        for p in range(6):
            hidden = silu(dot(source, win_ref[p]) + bias)
            if p == 0:
                hidden = jnp.where(top, 0.0, hidden)
            if p == 5:
                hidden = jnp.where(bottom, 0.0, hidden)
            h1[p, GRP : GRP + W] = hidden.astype(BF16)
            before = pltpu.roll(hidden[W - GRP :], 1, 0)
            h1[p, :GRP] = jnp.where(edge_row > 0, before, 0.0).astype(BF16)
            after = pltpu.roll(hidden[:GRP], GRP - 1, 0)
            h1[p, GRP + W :] = jnp.where(edge_row < GRP - 1, after, 0.0).astype(BF16)
        lane = lax.broadcasted_iota(jnp.int32, (W, 2 * C), 1)
        for j in range(5):
            windows = jnp.concatenate(
                [h1[j + n, GRP * d : GRP * d + W] for d in range(3) for n in range(2)], axis=1
            )
            kept = jnp.concatenate(
                [h1[j, GRP : GRP + W, C:], h1[j + 1, GRP : GRP + W, :C]], axis=1
            ).astype(F32)
            hidden = kept + silu(dot(windows, wmid_ref[...]))
            if j == 0:
                hidden = jnp.where(jnp.logical_and(top, lane < C), 0.0, hidden)
            if j == 4:
                hidden = jnp.where(jnp.logical_and(bottom, lane >= C), 0.0, hidden)
            h2[:, 2 * C * j : 2 * C * (j + 1)] = hidden.astype(BF16)
        product = dot_nt(wout_ref[...], h2[...])
        high = product.astype(BF16)
        low = (product - high.astype(F32)).astype(BF16)
        product = dot(high, perm[...]) + dot(low, perm[...])
        for b in range(B):
            score = 0.0
            for d in range(3):
                at = (d * B + b) * R
                score = score + shifted(product[at : at + R], d - 1)
            drift = (
                step_ref[t] * (score + guidance[t * B + b]) + scale_ref[t] * noise_ref[t, b]
            )
            running[b] = drift if t == 0 else running[b] + drift
            loc_ref[t, b] = start_ref[b] + running[b]
            if t == TH - 1:
                tot_ref[b] = running[b]


def weights_in(kernel):
    taps = kernel.reshape(3, 3, C, B).transpose(1, 3, 0, 2)
    pairs = []
    for p in range(6):
        subs = []
        for s in range(2):
            lead = 1 + 2 * p + s
            subs.append(jnp.pad(taps, ((0, 0), (0, 0), (lead, 2 * R - 3 - lead), (0, 0))))
        pairs.append(jnp.stack(subs, axis=3).reshape(3 * B * 2 * R, 2 * C))
    return jnp.stack(pairs)


def weights_mid(kernel):
    taps = kernel.reshape(3, 3, C, C).transpose(1, 0, 3, 2)
    subs = [jnp.pad(taps, ((0, 0), (s, 1 - s), (0, 0), (0, 0))) for s in range(2)]
    return jnp.stack(subs, axis=3).reshape(3 * 4 * C, 2 * C)


def weights_out(kernel):
    taps = kernel.reshape(3, 3, B, C).transpose(1, 2, 0, 3)
    rows = [jnp.pad(taps, ((0, 0), (0, 0), (r, 7 - r), (0, 0))) for r in range(R)]
    return jnp.stack(rows, axis=2).reshape(3 * B * R, 10 * C)


def per_device(
    trajectory, noise, step_size, noise_scale, time_bias, start_state, observed,
    conv_in, conv_mid, conv_out, psf_bank, index_map,
):
    vmem = pl.BlockSpec(memory_space=pltpu.VMEM)
    smem = pl.BlockSpec(memory_space=pltpu.SMEM)
    packed = jax.ShapeDtypeStruct((PACK, W), BF16)
    send_a, send_b = pl.pallas_call(
        pack_kernel,
        out_shape=(packed, packed),
        in_specs=[vmem, vmem],
        out_specs=(vmem, vmem),
        scratch_shapes=[pltpu.VMEM((PACK, W), F32)] * 2,
    )(trajectory, observed)

    n = lax.axis_size("space")
    swap_a = [(i, i ^ 1) for i in range(n)]
    swap_b = [(i, i) if i in (0, n - 1) else (i, ((i + 1) ^ 1) - 1) for i in range(n)]
    got_b = lax.ppermute(send_b, "space", swap_b)
    got_a = lax.ppermute(send_a, "space", swap_a)

    psf = psf_bank.reshape(NPSF, 25 * B).T
    psf = jnp.pad(psf, ((0, 4), (0, 0)))
    local = jax.ShapeDtypeStruct((TH, B, R, W), F32)
    total = jax.ShapeDtypeStruct((B, R, W), F32)
    loc, tot = pl.pallas_call(
        main_kernel,
        out_shape=(local, total),
        in_specs=[vmem, vmem, smem, smem] + [vmem] * 10,
        out_specs=(vmem, vmem),
        scratch_shapes=[
            pltpu.VMEM((TH * B, 3 * R, W), F32),
            pltpu.VMEM((5, TH * B, 3 * R, W), F32),
            pltpu.VMEM((B, 2 * R, W), F32),
            pltpu.VMEM((TH * B, 2 * R, W), F32),
            pltpu.VMEM((3, 104, W), F32),
            pltpu.VMEM((W, W), BF16),
            pltpu.VMEM((6, W + 2 * GRP, 2 * C), BF16),
            pltpu.VMEM((W, 10 * C), BF16),
            pltpu.VMEM((2, PACK, W), F32),
        ],
        compiler_params=pltpu.CompilerParams(vmem_limit_bytes=48 * 1024 * 1024),
    )(
        trajectory, noise, step_size, noise_scale, time_bias, start_state, observed,
        got_a, got_b, weights_in(conv_in), weights_mid(conv_mid), weights_out(conv_out),
        psf, index_map,
    )

    m = lax.axis_size("tm")
    me = lax.axis_index("tm")
    before = 0.0
    for k in range(1, m):
        part = lax.ppermute(tot, "tm", [(i, (i + k) % m) for i in range(m)])
        before = before + jnp.where(me >= k, part, 0.0)
    return loc + before


def solution(mesh):
    return jax.shard_map(
        per_device,
        mesh=mesh,
        in_specs=(
            P("tm", None, "space", None),
            P("tm", None, "space", None),
            P("tm"),
            P("tm"),
            P("tm", None),
            P(None, "space", None),
            P(None, "space", None),
            P(),
            P(),
            P(),
            P(),
            P(),
        ),
        out_specs=P("tm", None, "space", None),
        check_vma=False,
    )
```

```python
import jax
import jax.numpy as jnp
from jax import lax
from jax.experimental import pallas as pl
from jax.experimental.pallas import tpu as pltpu
from jax.sharding import PartitionSpec as P

F32 = jnp.float32
BF16 = jnp.bfloat16
B = 4
R = 8
W = 512
C = 128
TH = 2
HALO = 4
OH = 2
PACK = TH * B * HALO + B * OH
LANES = 128
GRP = 16
STR = W // GRP
NPSF = 16
MIB = 1024 * 1024
TAP_ROWS = 3 * B * 2 * R
NT = (((1,), (1,)), ((), ()))


def dot(a, b):
    return jnp.dot(a, b, preferred_element_type=F32)


def dot_nt(a, b):
    return lax.dot_general(a, b, NT, preferred_element_type=F32)


def dot_tn(a, b):
    return lax.dot_general(a, b, (((0,), (0,)), ((), ())), preferred_element_type=F32)


def silu_of_half(half):
    return half + half * jnp.tanh(half)


def shifted(v, by):
    if by == 0:
        return v
    lane = lax.broadcasted_iota(jnp.int32, v.shape, v.ndim - 1)
    moved = pltpu.roll(v, (-by) % W, v.ndim - 1)
    inside = lane < W - by if by > 0 else lane >= -by
    return jnp.where(inside, moved, 0.0)


def pack_kernel(x_hbm, obs_hbm, f_ref, s_ref, b_ref, x, obs, head, tail, sems):
    copies = [
        pltpu.make_async_copy(x_hbm, x, sems.at[0]),
        pltpu.make_async_copy(obs_hbm, obs, sems.at[1]),
    ]
    for copy in copies:
        copy.start()
    second = lax.axis_index("space") == 1
    for copy in copies:
        copy.wait()
    for t in range(TH):
        for b in range(B):
            at = (t * B + b) * HALO
            head[at : at + HALO] = x[t, b, :HALO]
            tail[at : at + HALO] = x[t, b, R - HALO :]
    for b in range(B):
        at = TH * B * HALO + b * OH
        head[at : at + OH] = obs[b, :OH]
        tail[at : at + OH] = obs[b, R - OH :]
    first, last = head[...], tail[...]
    f_ref[...] = jnp.where(second, first, last).astype(BF16)
    rest = jnp.where(second, last, first).astype(BF16)
    s_ref[...] = rest
    b_ref[...] = rest


def tables_kernel(
    psf_ref, map_ref, bias_ref, step_ref, scale_ref, perm_ref, wts_ref, rate_ref, bank
):
    place = lax.axis_index("space")

    count = map_ref.shape[0]
    blocks = [map_ref[pl.ds(jnp.clip(place + n - 1, 0, count - 1), 1), :] for n in range(3)]
    blocks = jnp.concatenate(blocks + [jnp.zeros((13, count), jnp.int32)], axis=0)
    spread = jnp.where(
        (lax.broadcasted_iota(jnp.int32, (count, W), 1) >> 3)
        == lax.broadcasted_iota(jnp.int32, (count, W), 0),
        1.0,
        0.0,
    ).astype(BF16)
    pixel = dot(blocks.astype(F32).astype(BF16), spread)
    kind = lax.broadcasted_iota(jnp.int32, (NPSF, W), 0).astype(F32)
    one_hot = jnp.concatenate(
        [jnp.where(pixel[n : n + 1] == kind, 1.0, 0.0) for n in range(3)], axis=1
    ).astype(BF16)
    bank[...] = jnp.zeros_like(bank)
    for b in range(B):
        bank[:, 32 * b : 32 * b + 25] = psf_ref[:, b, :]
    psf = bank[...]
    high = psf.astype(BF16)
    rest = psf - high.astype(F32)
    mid = rest.astype(BF16)
    low = (rest - mid.astype(F32)).astype(BF16)
    picked = dot_tn(
        jnp.concatenate([high, mid, low], axis=0), jnp.concatenate([one_hot] * 3, axis=0)
    )
    for n in range(3):
        wts_ref[n] = picked[:, n * W : (n + 1) * W]

    q = lax.broadcasted_iota(jnp.int32, (W, 1), 0)
    c = lax.broadcasted_iota(jnp.int32, (W, W), 1)
    perm_ref[...] = jnp.where((q & (GRP - 1)) * STR + (q >> 4) == c, 1.0, 0.0).astype(BF16)

    for t in range(TH):
        rate_ref[t : t + 1, :] = jnp.full((1, W), step_ref[t], F32)
        rate_ref[TH + t : TH + t + 1, :] = jnp.full((1, W), scale_ref[t], F32)
        rate_ref[2 * TH + t : 2 * TH + t + 1, :C] = bias_ref[t : t + 1, :]


def weights_kernel(
    win_raw, wmid_raw, wout_raw, rate_ref, win_ref, wmid_ref, wout_ref, wide, tall
):
    wide[...] = jnp.zeros_like(wide)
    for tap in range(9):
        dy, dx = tap // 3, tap % 3
        rows = 0.5 * win_raw[tap].astype(F32)
        for p in range(6):
            for s in range(2):
                for b in range(B):
                    at = (dx * B + b) * 2 * R + dy + 1 + 2 * p + s
                    wide[p, at : at + 1, s * C : (s + 1) * C] = rows[b : b + 1]
    for t in range(TH):
        rest = 0.5 * rate_ref[2 * TH + t : 2 * TH + t + 1, :C]
        for n in range(3):
            part = rest.astype(BF16).astype(F32)
            rest = rest - part
            at = TAP_ROWS + 3 * t + n
            for p in range(6):
                wide[p, at : at + 1, :C] = part
                wide[p, at : at + 1, C:] = part
    for p in range(6):
        win_ref[p] = wide[p].astype(BF16)

    for dx in range(3):
        for s in range(2):
            at = (dx * 4 + 3 * (1 - s)) * C
            wmid_ref[at : at + C, s * C : (s + 1) * C] = jnp.zeros((C, C), BF16)
        for dy in range(3):
            block = (0.5 * wmid_raw[dy * 3 + dx].astype(F32)).T.astype(BF16)
            for s in range(2):
                at = (dx * 4 + dy + s) * C
                wmid_ref[at : at + C, s * C : (s + 1) * C] = block

    tall[...] = jnp.zeros_like(tall)
    for tap in range(9):
        dy, dx = tap // 3, tap % 3
        rows = wout_raw[tap].astype(F32)
        for b in range(B):
            for r in range(R):
                at = (dx * B + b) * R + r
                tall[at : at + 1, (r + dy) * C : (r + dy + 1) * C] = rows[b : b + 1]
    wout_ref[...] = tall[...].T.astype(BF16)


def main_kernel(
    x_ref, noise_ref, start_ref, obs_ref, f_ref, s_ref, b_ref,
    win_ref, wmid_ref, wout_ref, perm, wts, rate_ref,
    loc_ref, tot_ref,
    xcol, obs, rows, mis, parts, src, h1, h2, halo,
):
    place = lax.axis_index("space")
    top = place == 0
    bottom = place == lax.axis_size("space") - 1

    got_f, got_s, got_b = (ref[...].astype(F32) for ref in (f_ref, s_ref, b_ref))
    halo[0] = jnp.where(top, 0.0, jnp.where(place == 2, got_s, got_f))
    below = jnp.where(top, got_f, jnp.where(place == 1, got_s, got_b))
    halo[1] = jnp.where(bottom, 0.0, below)
    for k in range(TH * B):
        xcol[2, k, 0:HALO] = halo[0, k * HALO : (k + 1) * HALO]
        xcol[2, k, HALO : HALO + R] = x_ref[k // B, k % B]
        xcol[2, k, HALO + R :] = halo[1, k * HALO : (k + 1) * HALO]
        for n in (0, 1, 3, 4):
            xcol[n, k] = shifted(xcol[2, k], n - 2)
    for b in range(B):
        at = TH * B * HALO + b * OH
        obs[b, 0:OH] = halo[0, at : at + OH]
        obs[b, OH : OH + R] = obs_ref[b]
        obs[b, OH + R : 2 * OH + R] = halo[1, at : at + OH]

    def source(t):
        taps = [xcol[n, t * B : (t + 1) * B].reshape(B * 2 * R, W) for n in (1, 2, 3)]
        line = lax.broadcasted_iota(jnp.int32, (2 * C - TAP_ROWS, W), 0)
        taps.append(jnp.where(jnp.logical_and(line >= 3 * t, line < 3 * t + 3), 1.0, 0.0))
        taps = jnp.concatenate(taps, axis=0).astype(BF16)
        src[t] = dot_nt(perm[...], taps).astype(BF16)

    edge_row = lax.broadcasted_iota(jnp.int32, (GRP, 2 * C), 0)

    def first(t, p):
        hidden = silu_of_half(dot(src[t], win_ref[p]))
        if p == 0:
            hidden = jnp.where(top, 0.0, hidden)
        if p == 5:
            hidden = jnp.where(bottom, 0.0, hidden)
        h1[t, p, GRP : GRP + W] = hidden.astype(BF16)
        before = pltpu.roll(hidden[W - GRP :], 1, 0)
        h1[t, p, :GRP] = jnp.where(edge_row > 0, before, 0.0).astype(BF16)
        after = pltpu.roll(hidden[:GRP], GRP - 1, 0)
        h1[t, p, GRP + W :] = jnp.where(edge_row < GRP - 1, after, 0.0).astype(BF16)

    lane = lax.broadcasted_iota(jnp.int32, (W, 2 * C), 1)

    def second(t, j):
        windows = jnp.concatenate(
            [h1[t, j + n, GRP * d : GRP * d + W] for d in range(3) for n in range(2)], axis=1
        )
        kept = jnp.concatenate(
            [h1[t, j, GRP : GRP + W, C:], h1[t, j + 1, GRP : GRP + W, :C]], axis=1
        ).astype(F32)
        hidden = kept + silu_of_half(dot(windows, wmid_ref[...]))
        if j == 0:
            hidden = jnp.where(jnp.logical_and(top, lane < C), 0.0, hidden)
        if j == 4:
            hidden = jnp.where(jnp.logical_and(bottom, lane >= C), 0.0, hidden)
        h2[t, :, 2 * C * j : 2 * C * (j + 1)] = hidden.astype(BF16)

    sub = lax.broadcasted_iota(jnp.int32, (R, LANES), 0)

    def blur(b):
        for at in range(0, W, LANES):
            cols = slice(at, at + LANES)
            for i in range(5):
                reach = sub < HALO + i - 2
                sums = [[0.0, 0.0] for _ in range(TH)]
                for j in range(5):
                    tap = 32 * b + 5 * i + j
                    up, own, down = (wts[n, tap : tap + 1, cols] for n in range(3))
                    w = (jnp.where(reach, up, own), jnp.where(reach, own, down))
                    for t in range(TH):
                        for n in range(2):
                            x = xcol[j, t * B + b, n * R : (n + 1) * R, cols]
                            sums[t][n] = sums[t][n] + w[n] * x
                for t in range(TH):
                    for n in range(2):
                        rows[t, i, n * R : (n + 1) * R, cols] = sums[t][n]
        inner = lax.broadcasted_iota(jnp.int32, (R + 2 * OH, W), 0)
        keep = jnp.logical_and(
            jnp.logical_or(inner >= OH, jnp.logical_not(top)),
            jnp.logical_or(inner < OH + R, jnp.logical_not(bottom)),
        )
        for t in range(TH):
            total = rows[t, 0, 0 : R + 2 * OH]
            for i in range(1, 5):
                total = total + rows[t, i, i : i + R + 2 * OH]
            mis[t * B + b] = jnp.where(keep, obs[b] - total, 0.0)

    guidance = {}

    def blur_back(b):
        for at in range(0, W, LANES):
            cols = slice(at, at + LANES)
            sums = [[0.0] * 5 for _ in range(TH)]
            for i in range(5):
                off = i - 2
                lines = [mis[t * B + b, OH - off : OH - off + R, cols] for t in range(TH)]
                for j in range(5):
                    tap = 32 * b + 5 * i + j
                    w = wts[1, tap : tap + 1, cols]
                    if off > 0:
                        w = jnp.where(sub < off, wts[0, tap : tap + 1, cols], w)
                    elif off < 0:
                        w = jnp.where(sub >= R + off, wts[2, tap : tap + 1, cols], w)
                    for t in range(TH):
                        sums[t][j] = sums[t][j] + w * lines[t]
            for t in range(TH):
                for j in range(5):
                    parts[t, j, :, cols] = sums[t][j]
        for t in range(TH):
            total = parts[t, 2]
            for j in (0, 1, 3, 4):
                total = total + shifted(parts[t, j], 2 - j)
            guidance[t, b] = total

    product = {}

    def third(t):
        both = dot(h2[t], wout_ref[...])
        high = both.astype(BF16)
        low = (both - high.astype(F32)).astype(BF16)
        product[t] = dot_tn(high, perm[...]) + dot_tn(low, perm[...])

    running = [None] * B

    def last(t):
        for b in range(B):
            score = 0.0
            for d in range(3):
                at = (d * B + b) * R
                score = score + shifted(product[t][at : at + R], d - 1)
            drift = (
                rate_ref[t : t + 1] * (score + guidance[t, b])
                + rate_ref[TH + t : TH + t + 1] * noise_ref[t, b]
            )
            running[b] = drift if t == 0 else running[b] + drift
            loc_ref[t, b] = start_ref[b] + running[b]
            if t == TH - 1:
                tot_ref[b] = running[b].astype(BF16)

    source(0)
    source(1)
    first(0, 0)
    first(0, 1)
    for t in range(TH):
        for j in range(5):
            second(t, j)
            if j < 4:
                first(t, j + 2)
            if j < B and t == 0:
                blur(j)
            if j == 1 and t == 1:
                third(0)
            if j < B and t == 1:
                blur_back(j)
        if t == 0:
            first(1, 0)
            first(1, 1)
    last(0)
    third(1)
    last(1)


def halo_routes(groups, count):
    def at(group, place):
        return group * count + place

    down, swap, up = [], [], []
    for g in range(groups):
        for i in range(count):
            other = at(g ^ 1, i)
            after = i + 1 if i < count - 1 else 2
            before = i - 1 if i > 2 else count - 1
            down.append((at(g, i), at(g, 1 - i if i < 2 else after)))
            swap.append((at(g, i), at(g, 3 - i) if i in (1, 2) else other))
            up.append((at(g, i), other if i < 2 else at(g, before)))
    return down, swap, up


def per_device(
    trajectory, noise, step_size, noise_scale, time_bias, start_state, observed,
    conv_in, conv_mid, conv_out, psf_bank, index_map,
):
    vmem = pl.BlockSpec(memory_space=pltpu.VMEM)
    smem = pl.BlockSpec(memory_space=pltpu.SMEM)
    hbm = pl.BlockSpec(memory_space=pltpu.HBM)
    packed = jax.ShapeDtypeStruct((PACK, W), BF16)
    send_f, send_s, send_b = pl.pallas_call(
        pack_kernel,
        out_shape=(packed, packed, packed),
        in_specs=[hbm, hbm],
        out_specs=(vmem, vmem, vmem),
        scratch_shapes=[
            pltpu.VMEM((TH, B, R, W), F32),
            pltpu.VMEM((B, R, W), F32),
            pltpu.VMEM((PACK, W), F32),
            pltpu.VMEM((PACK, W), F32),
            pltpu.SemaphoreType.DMA((2,)),
        ],
        cost_estimate=pl.CostEstimate(flops=2000000000, bytes_accessed=1000000, transcendentals=0),
        compiler_params=pltpu.CompilerParams(vmem_limit_bytes=60 * MIB),
    )(trajectory, observed)

    both = ("tm", "space")
    down, swap, up = halo_routes(lax.axis_size("tm"), lax.axis_size("space"))
    got_f = lax.ppermute(send_f, both, down)
    got_s = lax.ppermute(send_s, both, swap)
    got_b = lax.ppermute(send_b, both, up)

    tables = pl.pallas_call(
        tables_kernel,
        out_shape=(
            jax.ShapeDtypeStruct((W, W), BF16),
            jax.ShapeDtypeStruct((3, 32 * B, W), F32),
            jax.ShapeDtypeStruct((8, W), F32),
        ),
        in_specs=[vmem] * 3 + [smem] * 2,
        out_specs=(vmem,) * 3,
        scratch_shapes=[pltpu.VMEM((NPSF, 32 * B), F32)],
        cost_estimate=pl.CostEstimate(flops=2000000000, bytes_accessed=1000000, transcendentals=0),
        compiler_params=pltpu.CompilerParams(vmem_limit_bytes=8 * MIB),
    )(psf_bank, index_map, time_bias, step_size, noise_scale)
    weights = pl.pallas_call(
        weights_kernel,
        out_shape=(
            jax.ShapeDtypeStruct((6, 2 * C, 2 * C), BF16),
            jax.ShapeDtypeStruct((12 * C, 2 * C), BF16),
            jax.ShapeDtypeStruct((10 * C, C), BF16),
        ),
        in_specs=[vmem] * 4,
        out_specs=(vmem,) * 3,
        scratch_shapes=[
            pltpu.VMEM((6, 2 * C, 2 * C), F32),
            pltpu.VMEM((C, 10 * C), F32),
        ],
        cost_estimate=pl.CostEstimate(flops=2000000000, bytes_accessed=1000000, transcendentals=0),
        compiler_params=pltpu.CompilerParams(vmem_limit_bytes=8 * MIB),
    )(conv_in.transpose(0, 2, 1), conv_mid, conv_out, tables[2])

    local = jax.ShapeDtypeStruct((TH, B, R, W), F32)
    total = jax.ShapeDtypeStruct((B, R, W), BF16)
    loc, tot = pl.pallas_call(
        main_kernel,
        out_shape=(local, total),
        in_specs=[vmem] * 13,
        out_specs=(vmem, vmem),
        scratch_shapes=[
            pltpu.VMEM((5, TH * B, 2 * R, W), F32),
            pltpu.VMEM((B, R + 2 * OH, W), F32),
            pltpu.VMEM((TH, 5, 2 * R, W), F32),
            pltpu.VMEM((TH * B, R + 2 * OH, W), F32),
            pltpu.VMEM((TH, 5, R, W), F32),
            pltpu.VMEM((TH, W, 2 * C), BF16),
            pltpu.VMEM((TH, 6, W + 2 * GRP, 2 * C), BF16),
            pltpu.VMEM((TH, W, 10 * C), BF16),
            pltpu.VMEM((2, PACK, W), F32),
        ],
        cost_estimate=pl.CostEstimate(flops=8000000000, bytes_accessed=1000000, transcendentals=0),
        compiler_params=pltpu.CompilerParams(vmem_limit_bytes=24 * MIB),
    )(trajectory, noise, start_state, observed, got_f, got_s, got_b, *weights, *tables)

    m = lax.axis_size("tm")
    me = lax.axis_index("tm")
    before = 0.0
    for k in range(1, m):
        part = lax.ppermute(tot, "tm", [(i, (i + k) % m) for i in range(m)])
        before = before + jnp.where(me >= k, part.astype(F32), 0.0)
    return loc + before


def solution(mesh):
    return jax.shard_map(
        per_device,
        mesh=mesh,
        in_specs=(
            P("tm", None, "space", None),
            P("tm", None, "space", None),
            P("tm"),
            P("tm"),
            P("tm", None),
            P(None, "space", None),
            P(None, "space", None),
            P(),
            P(),
            P(),
            P(),
            P(),
        ),
        out_specs=P("tm", None, "space", None),
        check_vma=False,
    )
```

```python
import jax
import jax.numpy as jnp
from jax import lax
from jax.experimental import pallas as pl
from jax.experimental.pallas import tpu as pltpu
from jax.sharding import PartitionSpec as P

F32 = jnp.float32
BF16 = jnp.bfloat16
B = 4
R = 8
W = 512
C = 128
TH = 2
HALO = 4
OH = 2
LANES = 128
GRP = 16
STR = W // GRP
NPSF = 16
MIB = 1024 * 1024
TAP_ROWS = 3 * B * 2 * R
NT = (((1,), (1,)), ((), ()))


def dot(a, b):
    return jnp.dot(a, b, preferred_element_type=F32)


def dot_nt(a, b):
    return lax.dot_general(a, b, NT, preferred_element_type=F32)


def dot_tn(a, b):
    return lax.dot_general(a, b, (((0,), (0,)), ((), ())), preferred_element_type=F32)


def silu_of_half(half):
    return half + half * jnp.tanh(half)


def shifted(v, by):
    if by == 0:
        return v
    lane = lax.broadcasted_iota(jnp.int32, v.shape, v.ndim - 1)
    moved = pltpu.roll(v, (-by) % W, v.ndim - 1)
    inside = lane < W - by if by > 0 else lane >= -by
    return jnp.where(inside, moved, 0.0)


def tables_kernel(
    psf_ref, map_ref, bias_ref, step_ref, scale_ref, perm_ref, wts_ref, rate_ref, bank
):
    place = lax.axis_index("space")

    count = map_ref.shape[0]
    blocks = [map_ref[pl.ds(jnp.clip(place + n - 1, 0, count - 1), 1), :] for n in range(3)]
    blocks = jnp.concatenate(blocks + [jnp.zeros((13, count), jnp.int32)], axis=0)
    spread = jnp.where(
        (lax.broadcasted_iota(jnp.int32, (count, W), 1) >> 3)
        == lax.broadcasted_iota(jnp.int32, (count, W), 0),
        1.0,
        0.0,
    ).astype(BF16)
    pixel = dot(blocks.astype(F32).astype(BF16), spread)
    kind = lax.broadcasted_iota(jnp.int32, (NPSF, W), 0).astype(F32)
    one_hot = jnp.concatenate(
        [jnp.where(pixel[n : n + 1] == kind, 1.0, 0.0) for n in range(3)], axis=1
    ).astype(BF16)
    bank[...] = jnp.zeros_like(bank)
    for b in range(B):
        bank[:, 32 * b : 32 * b + 25] = psf_ref[:, b, :]
    psf = bank[...]
    high = psf.astype(BF16)
    rest = psf - high.astype(F32)
    mid = rest.astype(BF16)
    low = (rest - mid.astype(F32)).astype(BF16)
    picked = dot_tn(
        jnp.concatenate([high, mid, low], axis=0), jnp.concatenate([one_hot] * 3, axis=0)
    )
    for n in range(3):
        wts_ref[n] = picked[:, n * W : (n + 1) * W]

    q = lax.broadcasted_iota(jnp.int32, (W, 1), 0)
    c = lax.broadcasted_iota(jnp.int32, (W, W), 1)
    perm_ref[...] = jnp.where((q & (GRP - 1)) * STR + (q >> 4) == c, 1.0, 0.0).astype(BF16)

    for t in range(TH):
        rate_ref[t : t + 1, :] = jnp.full((1, W), step_ref[t], F32)
        rate_ref[TH + t : TH + t + 1, :] = jnp.full((1, W), scale_ref[t], F32)
        rate_ref[2 * TH + t : 2 * TH + t + 1, :C] = bias_ref[t : t + 1, :]


def weights_kernel(
    win_raw, wmid_raw, wout_raw, rate_ref, win_ref, wmid_ref, wout_ref, wide, tall
):
    wide[...] = jnp.zeros_like(wide)
    for tap in range(9):
        dy, dx = tap // 3, tap % 3
        rows = 0.5 * win_raw[tap].astype(F32)
        for p in range(6):
            for s in range(2):
                for b in range(B):
                    at = (dx * B + b) * 2 * R + dy + 1 + 2 * p + s
                    wide[p, at : at + 1, s * C : (s + 1) * C] = rows[b : b + 1]
    for t in range(TH):
        rest = 0.5 * rate_ref[2 * TH + t : 2 * TH + t + 1, :C]
        for n in range(3):
            part = rest.astype(BF16).astype(F32)
            rest = rest - part
            at = TAP_ROWS + 3 * t + n
            for p in range(6):
                wide[p, at : at + 1, :C] = part
                wide[p, at : at + 1, C:] = part
    for p in range(6):
        win_ref[p] = wide[p].astype(BF16)

    for dx in range(3):
        for s in range(2):
            at = (dx * 4 + 3 * (1 - s)) * C
            wmid_ref[at : at + C, s * C : (s + 1) * C] = jnp.zeros((C, C), BF16)
        for dy in range(3):
            block = (0.5 * wmid_raw[dy * 3 + dx].astype(F32)).T.astype(BF16)
            for s in range(2):
                at = (dx * 4 + dy + s) * C
                wmid_ref[at : at + C, s * C : (s + 1) * C] = block

    tall[...] = jnp.zeros_like(tall)
    for tap in range(9):
        dy, dx = tap // 3, tap % 3
        rows = wout_raw[tap].astype(F32)
        for b in range(B):
            for r in range(R):
                at = (dx * B + b) * R + r
                tall[at : at + 1, (r + dy) * C : (r + dy + 1) * C] = rows[b : b + 1]
    wout_ref[...] = tall[...].T.astype(BF16)


def main_kernel(
    x_ref, noise_ref, start_ref, obs_ref, f_ref, s_ref, b_ref,
    win_ref, wmid_ref, wout_ref, perm, wts, rate_ref,
    loc_ref, tot_ref,
    xcol, obs, rows, mis, parts, src, h1, h2, halo,
):
    place = lax.axis_index("space")
    top = place == 0
    bottom = place == lax.axis_size("space") - 1

    got_f, got_s, got_b = (ref[...].astype(F32) for ref in (f_ref, s_ref, b_ref))
    halo[0] = jnp.where(top, 0.0, jnp.where(place == 2, got_s, got_f))
    below = jnp.where(top, got_f, jnp.where(place == 1, got_s, got_b))
    halo[1] = jnp.where(bottom, 0.0, below)
    for k in range(TH * B):
        xcol[2, k, 0:HALO] = halo[0, k]
        xcol[2, k, HALO : HALO + R] = x_ref[k // B, k % B]
        xcol[2, k, HALO + R :] = halo[1, k]
        for n in (1, 3):
            xcol[n, k] = shifted(xcol[2, k], n - 2)
    for b in range(B):
        obs[b, 0:OH] = halo[0, TH * B + b, HALO - OH :]
        obs[b, OH : OH + R] = obs_ref[b]
        obs[b, OH + R : 2 * OH + R] = halo[1, TH * B + b, :OH]

    def source(t):
        taps = [xcol[n, t * B : (t + 1) * B].reshape(B * 2 * R, W) for n in (1, 2, 3)]
        line = lax.broadcasted_iota(jnp.int32, (2 * C - TAP_ROWS, W), 0)
        taps.append(jnp.where(jnp.logical_and(line >= 3 * t, line < 3 * t + 3), 1.0, 0.0))
        taps = jnp.concatenate(taps, axis=0).astype(BF16)
        src[t] = dot_nt(perm[...], taps).astype(BF16)

    edge_row = lax.broadcasted_iota(jnp.int32, (GRP, 2 * C), 0)

    def first(t, p):
        hidden = silu_of_half(dot(src[t], win_ref[p]))
        if p == 0:
            hidden = jnp.where(top, 0.0, hidden)
        if p == 5:
            hidden = jnp.where(bottom, 0.0, hidden)
        h1[t, p, GRP : GRP + W] = hidden.astype(BF16)
        before = pltpu.roll(hidden[W - GRP :], 1, 0)
        h1[t, p, :GRP] = jnp.where(edge_row > 0, before, 0.0).astype(BF16)
        after = pltpu.roll(hidden[:GRP], GRP - 1, 0)
        h1[t, p, GRP + W :] = jnp.where(edge_row < GRP - 1, after, 0.0).astype(BF16)

    lane = lax.broadcasted_iota(jnp.int32, (W, 2 * C), 1)

    def second(t, j):
        windows = jnp.concatenate(
            [h1[t, j + n, GRP * d : GRP * d + W] for d in range(3) for n in range(2)], axis=1
        )
        kept = jnp.concatenate(
            [h1[t, j, GRP : GRP + W, C:], h1[t, j + 1, GRP : GRP + W, :C]], axis=1
        ).astype(F32)
        hidden = kept + silu_of_half(dot(windows, wmid_ref[...]))
        if j == 0:
            hidden = jnp.where(jnp.logical_and(top, lane < C), 0.0, hidden)
        if j == 4:
            hidden = jnp.where(jnp.logical_and(bottom, lane >= C), 0.0, hidden)
        h2[t, :, 2 * C * j : 2 * C * (j + 1)] = hidden.astype(BF16)

    sub = lax.broadcasted_iota(jnp.int32, (R, LANES), 0)

    def blur(b):
        for at in range(0, W, LANES):
            cols = slice(at, at + LANES)
            for i in range(5):
                reach = sub < HALO + i - 2
                sums = [[0.0, 0.0] for _ in range(TH)]
                for j in range(5):
                    tap = 32 * b + 5 * i + j
                    up, own, down = (wts[n, tap : tap + 1, cols] for n in range(3))
                    w = (jnp.where(reach, up, own), jnp.where(reach, own, down))
                    for t in range(TH):
                        for n in range(2):
                            x = xcol[j, t * B + b, n * R : (n + 1) * R, cols]
                            sums[t][n] = sums[t][n] + w[n] * x
                for t in range(TH):
                    for n in range(2):
                        rows[t, i, n * R : (n + 1) * R, cols] = sums[t][n]
        inner = lax.broadcasted_iota(jnp.int32, (R + 2 * OH, W), 0)
        keep = jnp.logical_and(
            jnp.logical_or(inner >= OH, jnp.logical_not(top)),
            jnp.logical_or(inner < OH + R, jnp.logical_not(bottom)),
        )
        for t in range(TH):
            total = rows[t, 0, 0 : R + 2 * OH]
            for i in range(1, 5):
                total = total + rows[t, i, i : i + R + 2 * OH]
            mis[t * B + b] = jnp.where(keep, obs[b] - total, 0.0)

    guidance = {}

    def blur_back(b):
        for at in range(0, W, LANES):
            cols = slice(at, at + LANES)
            sums = [[0.0] * 5 for _ in range(TH)]
            for i in range(5):
                off = i - 2
                lines = [mis[t * B + b, OH - off : OH - off + R, cols] for t in range(TH)]
                for j in range(5):
                    tap = 32 * b + 5 * i + j
                    w = wts[1, tap : tap + 1, cols]
                    if off > 0:
                        w = jnp.where(sub < off, wts[0, tap : tap + 1, cols], w)
                    elif off < 0:
                        w = jnp.where(sub >= R + off, wts[2, tap : tap + 1, cols], w)
                    for t in range(TH):
                        sums[t][j] = sums[t][j] + w * lines[t]
            for t in range(TH):
                for j in range(5):
                    parts[t, j, :, cols] = sums[t][j]
        for t in range(TH):
            total = parts[t, 2]
            for j in (0, 1, 3, 4):
                total = total + shifted(parts[t, j], 2 - j)
            guidance[t, b] = total

    product = {}

    def third(t):
        both = dot(h2[t], wout_ref[...])
        high = both.astype(BF16)
        low = (both - high.astype(F32)).astype(BF16)
        product[t] = dot_tn(high, perm[...]) + dot_tn(low, perm[...])

    running = [None] * B

    def last(t):
        for b in range(B):
            score = 0.0
            for d in range(3):
                at = (d * B + b) * R
                score = score + shifted(product[t][at : at + R], d - 1)
            drift = (
                rate_ref[t : t + 1] * (score + guidance[t, b])
                + rate_ref[TH + t : TH + t + 1] * noise_ref[t, b]
            )
            running[b] = drift if t == 0 else running[b] + drift
            loc_ref[t, b] = start_ref[b] + running[b]
            if t == TH - 1:
                tot_ref[b] = running[b].astype(BF16)

    source(0)
    source(1)
    first(0, 0)
    first(0, 1)
    for k in range(TH * B):
        for n in (0, 4):
            xcol[n, k] = shifted(xcol[2, k], n - 2)
    for t in range(TH):
        for j in range(5):
            second(t, j)
            if j < 4:
                first(t, j + 2)
            if j < B and t == 0:
                blur(j)
            if j == 1 and t == 1:
                third(0)
            if j < B and t == 1:
                blur_back(j)
        if t == 0:
            first(1, 0)
            first(1, 1)
    last(0)
    third(1)
    last(1)


def halo_routes(groups, count):
    def at(group, place):
        return group * count + place

    down, swap, up = [], [], []
    for g in range(groups):
        for i in range(count):
            other = at(g ^ 1, i)
            after = i + 1 if i < count - 1 else 2
            before = i - 1 if i > 2 else count - 1
            down.append((at(g, i), at(g, 1 - i if i < 2 else after)))
            swap.append((at(g, i), at(g, 3 - i) if i in (1, 2) else other))
            up.append((at(g, i), other if i < 2 else at(g, before)))
    return down, swap, up


def per_device(
    trajectory, noise, step_size, noise_scale, time_bias, start_state, observed,
    conv_in, conv_mid, conv_out, psf_bank, index_map,
):
    vmem = pl.BlockSpec(memory_space=pltpu.VMEM)
    smem = pl.BlockSpec(memory_space=pltpu.SMEM)
    second = lax.axis_index("space") == 1
    cells = jnp.concatenate([trajectory.reshape(TH * B, R, W), observed])
    head, tail = cells[:, :HALO], cells[:, R - HALO :]
    send_f = jnp.where(second, head, tail).astype(BF16)
    send_s = jnp.where(second, tail, head).astype(BF16)
    send_b = head.astype(BF16)

    both = ("tm", "space")
    down, swap, up = halo_routes(lax.axis_size("tm"), lax.axis_size("space"))
    got_f = lax.ppermute(send_f, both, down)
    got_s = lax.ppermute(send_s, both, swap)
    got_b = lax.ppermute(send_b, both, up)

    tables = pl.pallas_call(
        tables_kernel,
        out_shape=(
            jax.ShapeDtypeStruct((W, W), BF16),
            jax.ShapeDtypeStruct((3, 32 * B, W), F32),
            jax.ShapeDtypeStruct((8, W), F32),
        ),
        in_specs=[vmem] * 3 + [smem] * 2,
        out_specs=(vmem,) * 3,
        scratch_shapes=[pltpu.VMEM((NPSF, 32 * B), F32)],
        cost_estimate=pl.CostEstimate(flops=2000000000, bytes_accessed=1000000, transcendentals=0),
        compiler_params=pltpu.CompilerParams(vmem_limit_bytes=8 * MIB),
    )(psf_bank, index_map, time_bias, step_size, noise_scale)
    weights = pl.pallas_call(
        weights_kernel,
        out_shape=(
            jax.ShapeDtypeStruct((6, 2 * C, 2 * C), BF16),
            jax.ShapeDtypeStruct((12 * C, 2 * C), BF16),
            jax.ShapeDtypeStruct((10 * C, C), BF16),
        ),
        in_specs=[vmem] * 4,
        out_specs=(vmem,) * 3,
        scratch_shapes=[
            pltpu.VMEM((6, 2 * C, 2 * C), F32),
            pltpu.VMEM((C, 10 * C), F32),
        ],
        cost_estimate=pl.CostEstimate(flops=2000000000, bytes_accessed=1000000, transcendentals=0),
        compiler_params=pltpu.CompilerParams(vmem_limit_bytes=8 * MIB),
    )(conv_in.transpose(0, 2, 1), conv_mid, conv_out, tables[2])

    local = jax.ShapeDtypeStruct((TH, B, R, W), F32)
    total = jax.ShapeDtypeStruct((B, R, W), BF16)
    loc, tot = pl.pallas_call(
        main_kernel,
        out_shape=(local, total),
        in_specs=[vmem] * 13,
        out_specs=(vmem, vmem),
        scratch_shapes=[
            pltpu.VMEM((5, TH * B, 2 * R, W), F32),
            pltpu.VMEM((B, R + 2 * OH, W), F32),
            pltpu.VMEM((TH, 5, 2 * R, W), F32),
            pltpu.VMEM((TH * B, R + 2 * OH, W), F32),
            pltpu.VMEM((TH, 5, R, W), F32),
            pltpu.VMEM((TH, W, 2 * C), BF16),
            pltpu.VMEM((TH, 6, W + 2 * GRP, 2 * C), BF16),
            pltpu.VMEM((TH, W, 10 * C), BF16),
            pltpu.VMEM((2, TH * B + B, HALO, W), F32),
        ],
        cost_estimate=pl.CostEstimate(flops=8000000000, bytes_accessed=1000000, transcendentals=0),
        compiler_params=pltpu.CompilerParams(vmem_limit_bytes=24 * MIB),
    )(trajectory, noise, start_state, observed, got_f, got_s, got_b, *weights, *tables)

    m = lax.axis_size("tm")
    me = lax.axis_index("tm")
    before = 0.0
    for k in range(1, m):
        part = lax.ppermute(tot, "tm", [(i, (i + k) % m) for i in range(m)])
        before = before + jnp.where(me >= k, part.astype(F32), 0.0)
    return loc + before


def solution(mesh):
    return jax.shard_map(
        per_device,
        mesh=mesh,
        in_specs=(
            P("tm", None, "space", None),
            P("tm", None, "space", None),
            P("tm"),
            P("tm"),
            P("tm", None),
            P(None, "space", None),
            P(None, "space", None),
            P(),
            P(),
            P(),
            P(),
            P(),
        ),
        out_specs=P("tm", None, "space", None),
        check_vma=False,
    )
```

```python
import jax
import jax.numpy as jnp
from jax import lax
from jax.experimental import pallas as pl
from jax.experimental.pallas import tpu as pltpu
from jax.sharding import PartitionSpec as P

F32 = jnp.float32
BF16 = jnp.bfloat16
B = 4
R = 8
W = 512
C = 128
TH = 2
HALO = 4
OH = 2
LANES = 128
GRP = 16
STR = W // GRP
NPSF = 16
MIB = 1024 * 1024
TAP_ROWS = 3 * B * 2 * R
NT = (((1,), (1,)), ((), ()))


def dot(a, b):
    return jnp.dot(a, b, preferred_element_type=F32)


def dot_nt(a, b):
    return lax.dot_general(a, b, NT, preferred_element_type=F32)


def dot_tn(a, b):
    return lax.dot_general(a, b, (((0,), (0,)), ((), ())), preferred_element_type=F32)


def silu_of_half(half):
    return half + half * jnp.tanh(half)


def shifted(v, by):
    if by == 0:
        return v
    lane = lax.broadcasted_iota(jnp.int32, v.shape, v.ndim - 1)
    moved = pltpu.roll(v, (-by) % W, v.ndim - 1)
    inside = lane < W - by if by > 0 else lane >= -by
    return jnp.where(inside, moved, 0.0)


def tables_kernel(
    psf_ref, map_ref, bias_ref, step_ref, scale_ref, perm_ref, wts_ref, rate_ref, bank
):
    place = lax.axis_index("space")

    count = map_ref.shape[0]
    blocks = [map_ref[pl.ds(jnp.clip(place + n - 1, 0, count - 1), 1), :] for n in range(3)]
    blocks = jnp.concatenate(blocks + [jnp.zeros((13, count), jnp.int32)], axis=0)
    spread = jnp.where(
        (lax.broadcasted_iota(jnp.int32, (count, W), 1) >> 3)
        == lax.broadcasted_iota(jnp.int32, (count, W), 0),
        1.0,
        0.0,
    ).astype(BF16)
    pixel = dot(blocks.astype(F32).astype(BF16), spread)
    kind = lax.broadcasted_iota(jnp.int32, (NPSF, W), 0).astype(F32)
    one_hot = jnp.concatenate(
        [jnp.where(pixel[n : n + 1] == kind, 1.0, 0.0) for n in range(3)], axis=1
    ).astype(BF16)
    bank[...] = jnp.zeros_like(bank)
    for b in range(B):
        bank[:, 32 * b : 32 * b + 25] = psf_ref[:, b, :]
    psf = bank[...]
    high = psf.astype(BF16)
    rest = psf - high.astype(F32)
    mid = rest.astype(BF16)
    low = (rest - mid.astype(F32)).astype(BF16)
    picked = dot_tn(
        jnp.concatenate([high, mid, low], axis=0), jnp.concatenate([one_hot] * 3, axis=0)
    )
    for n in range(3):
        wts_ref[n] = picked[:, n * W : (n + 1) * W]

    q = lax.broadcasted_iota(jnp.int32, (W, 1), 0)
    c = lax.broadcasted_iota(jnp.int32, (W, W), 1)
    perm_ref[...] = jnp.where((q & (GRP - 1)) * STR + (q >> 4) == c, 1.0, 0.0).astype(BF16)

    for t in range(TH):
        rate_ref[t : t + 1, :] = jnp.full((1, W), step_ref[t], F32)
        rate_ref[TH + t : TH + t + 1, :] = jnp.full((1, W), scale_ref[t], F32)
        rate_ref[2 * TH + t : 2 * TH + t + 1, :C] = bias_ref[t : t + 1, :]


def weights_kernel(
    win_raw, wmid_raw, wout_raw, rate_ref, win_ref, wmid_ref, wout_ref, wide, tall
):
    wide[...] = jnp.zeros_like(wide)
    for tap in range(9):
        dy, dx = tap // 3, tap % 3
        rows = 0.5 * win_raw[tap].astype(F32)
        for p in range(6):
            for s in range(2):
                for b in range(B):
                    at = (dx * B + b) * 2 * R + dy + 1 + 2 * p + s
                    wide[p, at : at + 1, s * C : (s + 1) * C] = rows[b : b + 1]
    for t in range(TH):
        rest = 0.5 * rate_ref[2 * TH + t : 2 * TH + t + 1, :C]
        for n in range(3):
            part = rest.astype(BF16).astype(F32)
            rest = rest - part
            at = TAP_ROWS + 3 * t + n
            for p in range(6):
                wide[p, at : at + 1, :C] = part
                wide[p, at : at + 1, C:] = part
    for p in range(6):
        win_ref[p] = wide[p].astype(BF16)

    for dx in range(3):
        for s in range(2):
            at = (dx * 4 + 3 * (1 - s)) * C
            wmid_ref[at : at + C, s * C : (s + 1) * C] = jnp.zeros((C, C), BF16)
        for dy in range(3):
            block = (0.5 * wmid_raw[dy * 3 + dx].astype(F32)).T.astype(BF16)
            for s in range(2):
                at = (dx * 4 + dy + s) * C
                wmid_ref[at : at + C, s * C : (s + 1) * C] = block

    tall[...] = jnp.zeros_like(tall)
    for tap in range(9):
        dy, dx = tap // 3, tap % 3
        rows = wout_raw[tap].astype(F32)
        for b in range(B):
            for r in range(R):
                at = (dx * B + b) * R + r
                tall[at : at + 1, (r + dy) * C : (r + dy + 1) * C] = rows[b : b + 1]
    wout_ref[...] = tall[...].T.astype(BF16)


def main_kernel(
    x_ref, noise_ref, start_ref, obs_ref, f_ref, s_ref, b_ref,
    win_ref, wmid_ref, wout_ref, perm, wts, rate_ref,
    loc_ref, tot_ref,
    xcol, obs, rows, mis, parts, src, h1, h2, halo,
):
    place = lax.axis_index("space")
    top = place == 0
    bottom = place == lax.axis_size("space") - 1

    got_f, got_s, got_b = (ref[...].astype(F32) for ref in (f_ref, s_ref, b_ref))
    halo[0] = jnp.where(top, 0.0, jnp.where(place == 2, got_s, got_f))
    below = jnp.where(top, got_f, jnp.where(place == 1, got_s, got_b))
    halo[1] = jnp.where(bottom, 0.0, below)
    for k in range(TH * B):
        xcol[2, k, 0:HALO] = halo[0, k]
        xcol[2, k, HALO : HALO + R] = x_ref[k // B, k % B]
        xcol[2, k, HALO + R :] = halo[1, k]
        for n in (1, 3):
            xcol[n, k] = shifted(xcol[2, k], n - 2)
    for b in range(B):
        obs[b, 0:OH] = halo[0, TH * B + b, HALO - OH :]
        obs[b, OH : OH + R] = obs_ref[b]
        obs[b, OH + R : 2 * OH + R] = halo[1, TH * B + b, :OH]

    def source(t):
        taps = [xcol[n, t * B : (t + 1) * B].reshape(B * 2 * R, W) for n in (1, 2, 3)]
        line = lax.broadcasted_iota(jnp.int32, (2 * C - TAP_ROWS, W), 0)
        taps.append(jnp.where(jnp.logical_and(line >= 3 * t, line < 3 * t + 3), 1.0, 0.0))
        taps = jnp.concatenate(taps, axis=0).astype(BF16)
        src[t] = dot_nt(perm[...], taps).astype(BF16)

    edge_row = lax.broadcasted_iota(jnp.int32, (GRP, 2 * C), 0)

    def first(t, p):
        hidden = silu_of_half(dot(src[t], win_ref[p]))
        if p == 0:
            hidden = jnp.where(top, 0.0, hidden)
        if p == 5:
            hidden = jnp.where(bottom, 0.0, hidden)
        h1[t, p, GRP : GRP + W] = hidden.astype(BF16)
        before = pltpu.roll(hidden[W - GRP :], 1, 0)
        h1[t, p, :GRP] = jnp.where(edge_row > 0, before, 0.0).astype(BF16)
        after = pltpu.roll(hidden[:GRP], GRP - 1, 0)
        h1[t, p, GRP + W :] = jnp.where(edge_row < GRP - 1, after, 0.0).astype(BF16)

    lane = lax.broadcasted_iota(jnp.int32, (W, 2 * C), 1)

    def second(t, j):
        windows = jnp.concatenate(
            [h1[t, j + n, GRP * d : GRP * d + W] for d in range(3) for n in range(2)], axis=1
        )
        kept = jnp.concatenate(
            [h1[t, j, GRP : GRP + W, C:], h1[t, j + 1, GRP : GRP + W, :C]], axis=1
        ).astype(F32)
        hidden = kept + silu_of_half(dot(windows, wmid_ref[...]))
        if j == 0:
            hidden = jnp.where(jnp.logical_and(top, lane < C), 0.0, hidden)
        if j == 4:
            hidden = jnp.where(jnp.logical_and(bottom, lane >= C), 0.0, hidden)
        h2[t, :, 2 * C * j : 2 * C * (j + 1)] = hidden.astype(BF16)

    sub = lax.broadcasted_iota(jnp.int32, (R, LANES), 0)

    def blur(b):
        for at in range(0, W, LANES):
            cols = slice(at, at + LANES)
            for i in range(5):
                reach = sub < HALO + i - 2
                sums = [[0.0, 0.0] for _ in range(TH)]
                for j in range(5):
                    tap = 32 * b + 5 * i + j
                    up, own, down = (wts[n, tap : tap + 1, cols] for n in range(3))
                    w = (jnp.where(reach, up, own), jnp.where(reach, own, down))
                    for t in range(TH):
                        for n in range(2):
                            x = xcol[j, t * B + b, n * R : (n + 1) * R, cols]
                            sums[t][n] = sums[t][n] + w[n] * x
                for t in range(TH):
                    for n in range(2):
                        rows[t, i, n * R : (n + 1) * R, cols] = sums[t][n]
        inner = lax.broadcasted_iota(jnp.int32, (R + 2 * OH, W), 0)
        keep = jnp.logical_and(
            jnp.logical_or(inner >= OH, jnp.logical_not(top)),
            jnp.logical_or(inner < OH + R, jnp.logical_not(bottom)),
        )
        for t in range(TH):
            total = rows[t, 0, 0 : R + 2 * OH]
            for i in range(1, 5):
                total = total + rows[t, i, i : i + R + 2 * OH]
            mis[t * B + b] = jnp.where(keep, obs[b] - total, 0.0)

    guidance = {}

    def blur_back(b):
        for at in range(0, W, LANES):
            cols = slice(at, at + LANES)
            sums = [[0.0] * 5 for _ in range(TH)]
            for i in range(5):
                off = i - 2
                lines = [mis[t * B + b, OH - off : OH - off + R, cols] for t in range(TH)]
                for j in range(5):
                    tap = 32 * b + 5 * i + j
                    w = wts[1, tap : tap + 1, cols]
                    if off > 0:
                        w = jnp.where(sub < off, wts[0, tap : tap + 1, cols], w)
                    elif off < 0:
                        w = jnp.where(sub >= R + off, wts[2, tap : tap + 1, cols], w)
                    for t in range(TH):
                        sums[t][j] = sums[t][j] + w * lines[t]
            for t in range(TH):
                for j in range(5):
                    parts[t, j, :, cols] = sums[t][j]
        for t in range(TH):
            total = parts[t, 2]
            for j in (0, 1, 3, 4):
                total = total + shifted(parts[t, j], 2 - j)
            guidance[t, b] = total

    product = {}

    def third(t):
        both = dot(h2[t], wout_ref[...])
        high = both.astype(BF16)
        low = (both - high.astype(F32)).astype(BF16)
        product[t] = dot_tn(high, perm[...]) + dot_tn(low, perm[...])

    running = [None] * B

    def last(t):
        for b in range(B):
            score = 0.0
            for d in range(3):
                at = (d * B + b) * R
                score = score + shifted(product[t][at : at + R], d - 1)
            drift = (
                rate_ref[t : t + 1] * (score + guidance[t, b])
                + rate_ref[TH + t : TH + t + 1] * noise_ref[t, b]
            )
            running[b] = drift if t == 0 else running[b] + drift
            loc_ref[t, b] = start_ref[b] + running[b]
            if t == TH - 1:
                tot_ref[b] = running[b].astype(BF16)

    source(0)
    source(1)
    first(0, 0)
    first(0, 1)
    for k in range(TH * B):
        for n in (0, 4):
            xcol[n, k] = shifted(xcol[2, k], n - 2)
    for t in range(TH):
        for j in range(5):
            second(t, j)
            if j < 4:
                first(t, j + 2)
            if j < B and t == 0:
                blur(j)
            if j == 1 and t == 1:
                third(0)
            if j < B and t == 1:
                blur_back(j)
        if t == 0:
            first(1, 0)
            first(1, 1)
    last(0)
    third(1)
    last(1)


def halo_routes(groups, count):
    def at(group, place):
        return group * count + place

    down, swap, up = [], [], []
    for g in range(groups):
        for i in range(count):
            other = at(g ^ 1, i)
            after = i + 1 if i < count - 1 else 2
            before = i - 1 if i > 2 else count - 1
            down.append((at(g, i), at(g, 1 - i if i < 2 else after)))
            swap.append((at(g, i), at(g, 3 - i) if i in (1, 2) else other))
            up.append((at(g, i), other if i < 2 else at(g, before)))
    return down, swap, up


def per_device(
    trajectory, noise, step_size, noise_scale, time_bias, start_state, observed,
    conv_in, conv_mid, conv_out, psf_bank, index_map,
):
    vmem = pl.BlockSpec(memory_space=pltpu.VMEM)
    smem = pl.BlockSpec(memory_space=pltpu.SMEM)
    second = lax.axis_index("space") == 1
    cells = jnp.concatenate([trajectory.reshape(TH * B, R, W), observed])
    head, tail = cells[:, :HALO], cells[:, R - HALO :]
    send_f = jnp.where(second, head, tail).astype(BF16)
    send_s = jnp.where(second, tail, head).astype(BF16)
    send_b = head.astype(BF16)

    both = ("tm", "space")
    down, swap, up = halo_routes(lax.axis_size("tm"), lax.axis_size("space"))
    got_f = lax.ppermute(send_f, both, down)
    got_s = lax.ppermute(send_s, both, swap)
    got_b = lax.ppermute(send_b, both, up)

    tables = pl.pallas_call(
        tables_kernel,
        out_shape=(
            jax.ShapeDtypeStruct((W, W), BF16),
            jax.ShapeDtypeStruct((3, 32 * B, W), F32),
            jax.ShapeDtypeStruct((8, W), F32),
        ),
        in_specs=[vmem] * 3 + [smem] * 2,
        out_specs=(vmem,) * 3,
        scratch_shapes=[pltpu.VMEM((NPSF, 32 * B), F32)],
        cost_estimate=pl.CostEstimate(flops=2000000000, bytes_accessed=1000000, transcendentals=0),
        compiler_params=pltpu.CompilerParams(vmem_limit_bytes=8 * MIB),
    )(psf_bank, index_map, time_bias, step_size, noise_scale)
    weights = pl.pallas_call(
        weights_kernel,
        out_shape=(
            jax.ShapeDtypeStruct((6, 2 * C, 2 * C), BF16),
            jax.ShapeDtypeStruct((12 * C, 2 * C), BF16),
            jax.ShapeDtypeStruct((10 * C, C), BF16),
        ),
        in_specs=[vmem] * 4,
        out_specs=(vmem,) * 3,
        scratch_shapes=[
            pltpu.VMEM((6, 2 * C, 2 * C), F32),
            pltpu.VMEM((C, 10 * C), F32),
        ],
        cost_estimate=pl.CostEstimate(flops=2000000000, bytes_accessed=1000000, transcendentals=0),
        compiler_params=pltpu.CompilerParams(vmem_limit_bytes=8 * MIB),
    )(conv_in.transpose(0, 2, 1), conv_mid, conv_out, tables[2])

    local = jax.ShapeDtypeStruct((TH, B, R, W), F32)
    total = jax.ShapeDtypeStruct((B, R, W), BF16)
    loc, tot = pl.pallas_call(
        main_kernel,
        out_shape=(local, total),
        in_specs=[vmem] * 13,
        out_specs=(vmem, vmem),
        scratch_shapes=[
            pltpu.VMEM((5, TH * B, 2 * R, W), F32),
            pltpu.VMEM((B, R + 2 * OH, W), F32),
            pltpu.VMEM((TH, 5, 2 * R, W), F32),
            pltpu.VMEM((TH * B, R + 2 * OH, W), F32),
            pltpu.VMEM((TH, 5, R, W), F32),
            pltpu.VMEM((TH, W, 2 * C), BF16),
            pltpu.VMEM((TH, 6, W + 2 * GRP, 2 * C), BF16),
            pltpu.VMEM((TH, W, 10 * C), BF16),
            pltpu.VMEM((2, TH * B + B, HALO, W), F32),
        ],
        cost_estimate=pl.CostEstimate(flops=8000000000, bytes_accessed=1000000, transcendentals=0),
        compiler_params=pltpu.CompilerParams(vmem_limit_bytes=24 * MIB),
    )(trajectory, noise, start_state, observed, got_f, got_s, got_b, *weights, *tables)

    m = lax.axis_size("tm")
    me = lax.axis_index("tm")
    before = 0.0
    for k in reversed(range(1, m)):
        part = lax.ppermute(tot, "tm", [(i, i ^ k) for i in range(m)])
        before = before + jnp.where(me > (me ^ k), part.astype(F32), 0.0)
    return loc + before


def solution(mesh):
    return jax.shard_map(
        per_device,
        mesh=mesh,
        in_specs=(
            P("tm", None, "space", None),
            P("tm", None, "space", None),
            P("tm"),
            P("tm"),
            P("tm", None),
            P(None, "space", None),
            P(None, "space", None),
            P(),
            P(),
            P(),
            P(),
            P(),
        ),
        out_specs=P("tm", None, "space", None),
        check_vma=False,
    )
```

```python
import jax
import jax.numpy as jnp
from jax import lax
from jax.experimental import pallas as pl
from jax.experimental.pallas import tpu as pltpu
from jax.sharding import PartitionSpec as P

F32 = jnp.float32
BF16 = jnp.bfloat16
B = 4
R = 8
W = 512
C = 128
TH = 2
HALO = 4
OH = 2
LANES = 128
GRP = 16
STR = W // GRP
NPSF = 16
MIB = 1024 * 1024
TAP_ROWS = 3 * B * 2 * R
NT = (((1,), (1,)), ((), ()))


def dot(a, b):
    return jnp.dot(a, b, preferred_element_type=F32)


def dot_nt(a, b):
    return lax.dot_general(a, b, NT, preferred_element_type=F32)


def dot_tn(a, b):
    return lax.dot_general(a, b, (((0,), (0,)), ((), ())), preferred_element_type=F32)


def silu_of_half(half):
    return half + half * jnp.tanh(half)


def shifted(v, by):
    if by == 0:
        return v
    lane = lax.broadcasted_iota(jnp.int32, v.shape, v.ndim - 1)
    moved = pltpu.roll(v, (-by) % W, v.ndim - 1)
    inside = lane < W - by if by > 0 else lane >= -by
    return jnp.where(inside, moved, 0.0)


def tables_kernel(
    psf_ref, map_ref, bias_ref, step_ref, scale_ref, perm_ref, wts_ref, rate_ref, bank
):
    place = lax.axis_index("space")

    count = map_ref.shape[0]
    blocks = [map_ref[pl.ds(jnp.clip(place + n - 1, 0, count - 1), 1), :] for n in range(3)]
    blocks = jnp.concatenate(blocks + [jnp.zeros((13, count), jnp.int32)], axis=0)
    spread = jnp.where(
        (lax.broadcasted_iota(jnp.int32, (count, W), 1) >> 3)
        == lax.broadcasted_iota(jnp.int32, (count, W), 0),
        1.0,
        0.0,
    ).astype(BF16)
    pixel = dot(blocks.astype(F32).astype(BF16), spread)
    kind = lax.broadcasted_iota(jnp.int32, (NPSF, W), 0).astype(F32)
    one_hot = jnp.concatenate(
        [jnp.where(pixel[n : n + 1] == kind, 1.0, 0.0) for n in range(3)], axis=1
    ).astype(BF16)
    bank[...] = jnp.zeros_like(bank)
    for b in range(B):
        bank[:, 32 * b : 32 * b + 25] = psf_ref[:, b, :]
    psf = bank[...]
    high = psf.astype(BF16)
    rest = psf - high.astype(F32)
    mid = rest.astype(BF16)
    low = (rest - mid.astype(F32)).astype(BF16)
    picked = dot_tn(
        jnp.concatenate([high, mid, low], axis=0), jnp.concatenate([one_hot] * 3, axis=0)
    )
    for n in range(3):
        wts_ref[n] = picked[:, n * W : (n + 1) * W]

    q = lax.broadcasted_iota(jnp.int32, (W, 1), 0)
    c = lax.broadcasted_iota(jnp.int32, (W, W), 1)
    perm_ref[...] = jnp.where((q & (GRP - 1)) * STR + (q >> 4) == c, 1.0, 0.0).astype(BF16)

    for t in range(TH):
        rate_ref[t : t + 1, :] = jnp.full((1, W), step_ref[t], F32)
        rate_ref[TH + t : TH + t + 1, :] = jnp.full((1, W), scale_ref[t], F32)
        rate_ref[2 * TH + t : 2 * TH + t + 1, :C] = bias_ref[t : t + 1, :]


def weights_kernel(
    win_raw, wmid_raw, wout_raw, rate_ref, win_ref, wmid_ref, wout_ref, wide, tall
):
    wide[...] = jnp.zeros_like(wide)
    for tap in range(9):
        dy, dx = tap // 3, tap % 3
        rows = 0.5 * win_raw[tap].astype(F32)
        for p in range(6):
            for s in range(2):
                for b in range(B):
                    at = (dx * B + b) * 2 * R + dy + 1 + 2 * p + s
                    wide[p, at : at + 1, s * C : (s + 1) * C] = rows[b : b + 1]
    for t in range(TH):
        rest = 0.5 * rate_ref[2 * TH + t : 2 * TH + t + 1, :C]
        for n in range(3):
            part = rest.astype(BF16).astype(F32)
            rest = rest - part
            at = TAP_ROWS + 3 * t + n
            for p in range(6):
                wide[p, at : at + 1, :C] = part
                wide[p, at : at + 1, C:] = part
    for p in range(6):
        win_ref[p] = wide[p].astype(BF16)

    for dx in range(3):
        for s in range(2):
            at = (dx * 4 + 3 * (1 - s)) * C
            wmid_ref[at : at + C, s * C : (s + 1) * C] = jnp.zeros((C, C), BF16)
        for dy in range(3):
            block = (0.5 * wmid_raw[dy * 3 + dx].astype(F32)).T.astype(BF16)
            for s in range(2):
                at = (dx * 4 + dy + s) * C
                wmid_ref[at : at + C, s * C : (s + 1) * C] = block

    tall[...] = jnp.zeros_like(tall)
    for tap in range(9):
        dy, dx = tap // 3, tap % 3
        rows = wout_raw[tap].astype(F32)
        for b in range(B):
            for r in range(R):
                at = (dx * B + b) * R + r
                tall[at : at + 1, (r + dy) * C : (r + dy + 1) * C] = rows[b : b + 1]
    wout_ref[...] = tall[...].T.astype(BF16)


def main_kernel(
    x_ref, noise_ref, start_ref, obs_ref, f_ref, s_ref, b_ref,
    win_ref, wmid_ref, wout_ref, perm, wts, rate_ref,
    loc_ref, tot_ref,
    xcol, obs, rows, mis, parts, src, h1, h2, halo,
):
    place = lax.axis_index("space")
    top = place == 0
    bottom = place == lax.axis_size("space") - 1

    got_f, got_s, got_b = (ref[...].astype(F32) for ref in (f_ref, s_ref, b_ref))
    halo[0] = jnp.where(top, 0.0, jnp.where(place == 2, got_s, got_f))
    below = jnp.where(top, got_f, jnp.where(place == 1, got_s, got_b))
    halo[1] = jnp.where(bottom, 0.0, below)
    for k in range(TH * B):
        xcol[2, k, 0:HALO] = halo[0, k]
        xcol[2, k, HALO : HALO + R] = x_ref[k // B, k % B]
        xcol[2, k, HALO + R :] = halo[1, k]
        for n in (1, 3):
            xcol[n, k] = shifted(xcol[2, k], n - 2)
    for b in range(B):
        obs[b, 0:OH] = halo[0, TH * B + b, HALO - OH :]
        obs[b, OH : OH + R] = obs_ref[b]
        obs[b, OH + R : 2 * OH + R] = halo[1, TH * B + b, :OH]

    def source(t):
        taps = [xcol[n, t * B : (t + 1) * B].reshape(B * 2 * R, W) for n in (1, 2, 3)]
        line = lax.broadcasted_iota(jnp.int32, (2 * C - TAP_ROWS, W), 0)
        taps.append(jnp.where(jnp.logical_and(line >= 3 * t, line < 3 * t + 3), 1.0, 0.0))
        taps = jnp.concatenate(taps, axis=0).astype(BF16)
        src[t] = dot_nt(perm[...], taps).astype(BF16)

    edge_row = lax.broadcasted_iota(jnp.int32, (GRP, 2 * C), 0)

    def first(t, p):
        hidden = silu_of_half(dot(src[t], win_ref[p]))
        if p == 0:
            hidden = jnp.where(top, 0.0, hidden)
        if p == 5:
            hidden = jnp.where(bottom, 0.0, hidden)
        h1[t, p, GRP : GRP + W] = hidden.astype(BF16)
        before = pltpu.roll(hidden[W - GRP :], 1, 0)
        h1[t, p, :GRP] = jnp.where(edge_row > 0, before, 0.0).astype(BF16)
        after = pltpu.roll(hidden[:GRP], GRP - 1, 0)
        h1[t, p, GRP + W :] = jnp.where(edge_row < GRP - 1, after, 0.0).astype(BF16)

    lane = lax.broadcasted_iota(jnp.int32, (W, 2 * C), 1)

    def second(t, j):
        windows = jnp.concatenate(
            [h1[t, j + n, GRP * d : GRP * d + W] for d in range(3) for n in range(2)], axis=1
        )
        kept = jnp.concatenate(
            [h1[t, j, GRP : GRP + W, C:], h1[t, j + 1, GRP : GRP + W, :C]], axis=1
        ).astype(F32)
        hidden = kept + silu_of_half(dot(windows, wmid_ref[...]))
        if j == 0:
            hidden = jnp.where(jnp.logical_and(top, lane < C), 0.0, hidden)
        if j == 4:
            hidden = jnp.where(jnp.logical_and(bottom, lane >= C), 0.0, hidden)
        h2[t, :, 2 * C * j : 2 * C * (j + 1)] = hidden.astype(BF16)

    sub = lax.broadcasted_iota(jnp.int32, (R, LANES), 0)

    def blur(b):
        for at in range(0, W, LANES):
            cols = slice(at, at + LANES)
            for i in range(5):
                reach = sub < HALO + i - 2
                sums = [[0.0, 0.0] for _ in range(TH)]
                for j in range(5):
                    tap = 32 * b + 5 * i + j
                    up, own, down = (wts[n, tap : tap + 1, cols] for n in range(3))
                    w = (jnp.where(reach, up, own), jnp.where(reach, own, down))
                    for t in range(TH):
                        for n in range(2):
                            x = xcol[j, t * B + b, n * R : (n + 1) * R, cols]
                            sums[t][n] = sums[t][n] + w[n] * x
                for t in range(TH):
                    for n in range(2):
                        rows[t, i, n * R : (n + 1) * R, cols] = sums[t][n]
        inner = lax.broadcasted_iota(jnp.int32, (R + 2 * OH, W), 0)
        keep = jnp.logical_and(
            jnp.logical_or(inner >= OH, jnp.logical_not(top)),
            jnp.logical_or(inner < OH + R, jnp.logical_not(bottom)),
        )
        for t in range(TH):
            total = rows[t, 0, 0 : R + 2 * OH]
            for i in range(1, 5):
                total = total + rows[t, i, i : i + R + 2 * OH]
            mis[t * B + b] = jnp.where(keep, obs[b] - total, 0.0)

    guidance = {}

    def blur_back(b):
        for at in range(0, W, LANES):
            cols = slice(at, at + LANES)
            sums = [[0.0] * 5 for _ in range(TH)]
            for i in range(5):
                off = i - 2
                lines = [mis[t * B + b, OH - off : OH - off + R, cols] for t in range(TH)]
                for j in range(5):
                    tap = 32 * b + 5 * i + j
                    w = wts[1, tap : tap + 1, cols]
                    if off > 0:
                        w = jnp.where(sub < off, wts[0, tap : tap + 1, cols], w)
                    elif off < 0:
                        w = jnp.where(sub >= R + off, wts[2, tap : tap + 1, cols], w)
                    for t in range(TH):
                        sums[t][j] = sums[t][j] + w * lines[t]
            for t in range(TH):
                for j in range(5):
                    parts[t, j, :, cols] = sums[t][j]
        for t in range(TH):
            total = parts[t, 2]
            for j in (0, 1, 3, 4):
                total = total + shifted(parts[t, j], 2 - j)
            guidance[t, b] = total

    product = {}

    def third(t):
        both = dot(h2[t], wout_ref[...])
        high = both.astype(BF16)
        low = (both - high.astype(F32)).astype(BF16)
        moved = dot_tn(jnp.concatenate([high, low], axis=1), perm[...])
        product[t] = moved[:C] + moved[C:]

    running = [None] * B

    def last(t):
        for b in range(B):
            score = 0.0
            for d in range(3):
                at = (d * B + b) * R
                score = score + shifted(product[t][at : at + R], d - 1)
            drift = (
                rate_ref[t : t + 1] * (score + guidance[t, b])
                + rate_ref[TH + t : TH + t + 1] * noise_ref[t, b]
            )
            running[b] = drift if t == 0 else running[b] + drift
            loc_ref[t, b] = start_ref[b] + running[b]
            if t == TH - 1:
                tot_ref[b] = running[b].astype(BF16)

    source(0)
    source(1)
    first(0, 0)
    first(0, 1)
    for k in range(TH * B):
        for n in (0, 4):
            xcol[n, k] = shifted(xcol[2, k], n - 2)
    for t in range(TH):
        for j in range(5):
            second(t, j)
            if j < 4:
                first(t, j + 2)
            if j < B and t == 0:
                blur(j)
            if j == 1 and t == 1:
                third(0)
            if j < B and t == 1:
                blur_back(j)
        if t == 0:
            first(1, 0)
            first(1, 1)
    last(0)
    third(1)
    last(1)


def halo_routes(groups, count):
    def at(group, place):
        return group * count + place

    down, swap, up = [], [], []
    for g in range(groups):
        for i in range(count):
            other = at(g ^ 1, i)
            after = i + 1 if i < count - 1 else 2
            before = i - 1 if i > 2 else count - 1
            down.append((at(g, i), at(g, 1 - i if i < 2 else after)))
            swap.append((at(g, i), at(g, 3 - i) if i in (1, 2) else other))
            up.append((at(g, i), other if i < 2 else at(g, before)))
    return down, swap, up


def per_device(
    trajectory, noise, step_size, noise_scale, time_bias, start_state, observed,
    conv_in, conv_mid, conv_out, psf_bank, index_map,
):
    vmem = pl.BlockSpec(memory_space=pltpu.VMEM)
    smem = pl.BlockSpec(memory_space=pltpu.SMEM)
    second = lax.axis_index("space") == 1
    cells = jnp.concatenate([trajectory.reshape(TH * B, R, W), observed])
    head, tail = cells[:, :HALO], cells[:, R - HALO :]
    send_f = jnp.where(second, head, tail).astype(BF16)
    send_s = jnp.where(second, tail, head).astype(BF16)
    send_b = head.astype(BF16)

    both = ("tm", "space")
    down, swap, up = halo_routes(lax.axis_size("tm"), lax.axis_size("space"))
    got_f = lax.ppermute(send_f, both, down)
    got_s = lax.ppermute(send_s, both, swap)
    got_b = lax.ppermute(send_b, both, up)

    tables = pl.pallas_call(
        tables_kernel,
        out_shape=(
            jax.ShapeDtypeStruct((W, W), BF16),
            jax.ShapeDtypeStruct((3, 32 * B, W), F32),
            jax.ShapeDtypeStruct((8, W), F32),
        ),
        in_specs=[vmem] * 3 + [smem] * 2,
        out_specs=(vmem,) * 3,
        scratch_shapes=[pltpu.VMEM((NPSF, 32 * B), F32)],
        cost_estimate=pl.CostEstimate(flops=2000000000, bytes_accessed=1000000, transcendentals=0),
        compiler_params=pltpu.CompilerParams(vmem_limit_bytes=8 * MIB),
    )(psf_bank, index_map, time_bias, step_size, noise_scale)
    weights = pl.pallas_call(
        weights_kernel,
        out_shape=(
            jax.ShapeDtypeStruct((6, 2 * C, 2 * C), BF16),
            jax.ShapeDtypeStruct((12 * C, 2 * C), BF16),
            jax.ShapeDtypeStruct((10 * C, C), BF16),
        ),
        in_specs=[vmem] * 4,
        out_specs=(vmem,) * 3,
        scratch_shapes=[
            pltpu.VMEM((6, 2 * C, 2 * C), F32),
            pltpu.VMEM((C, 10 * C), F32),
        ],
        cost_estimate=pl.CostEstimate(flops=2000000000, bytes_accessed=1000000, transcendentals=0),
        compiler_params=pltpu.CompilerParams(vmem_limit_bytes=8 * MIB),
    )(conv_in.transpose(0, 2, 1), conv_mid, conv_out, tables[2])

    local = jax.ShapeDtypeStruct((TH, B, R, W), F32)
    total = jax.ShapeDtypeStruct((B, R, W), BF16)
    loc, tot = pl.pallas_call(
        main_kernel,
        out_shape=(local, total),
        in_specs=[vmem] * 13,
        out_specs=(vmem, vmem),
        scratch_shapes=[
            pltpu.VMEM((5, TH * B, 2 * R, W), F32),
            pltpu.VMEM((B, R + 2 * OH, W), F32),
            pltpu.VMEM((TH, 5, 2 * R, W), F32),
            pltpu.VMEM((TH * B, R + 2 * OH, W), F32),
            pltpu.VMEM((TH, 5, R, W), F32),
            pltpu.VMEM((TH, W, 2 * C), BF16),
            pltpu.VMEM((TH, 6, W + 2 * GRP, 2 * C), BF16),
            pltpu.VMEM((TH, W, 10 * C), BF16),
            pltpu.VMEM((2, TH * B + B, HALO, W), F32),
        ],
        cost_estimate=pl.CostEstimate(flops=8000000000, bytes_accessed=1000000, transcendentals=0),
        compiler_params=pltpu.CompilerParams(vmem_limit_bytes=24 * MIB),
    )(trajectory, noise, start_state, observed, got_f, got_s, got_b, *weights, *tables)

    m = lax.axis_size("tm")
    me = lax.axis_index("tm")
    before = 0.0
    for k in reversed(range(1, m)):
        part = lax.ppermute(tot, "tm", [(i, i ^ k) for i in range(m)])
        before = before + jnp.where(me > (me ^ k), part.astype(F32), 0.0)
    return loc + before


def solution(mesh):
    return jax.shard_map(
        per_device,
        mesh=mesh,
        in_specs=(
            P("tm", None, "space", None),
            P("tm", None, "space", None),
            P("tm"),
            P("tm"),
            P("tm", None),
            P(None, "space", None),
            P(None, "space", None),
            P(),
            P(),
            P(),
            P(),
            P(),
        ),
        out_specs=P("tm", None, "space", None),
        check_vma=False,
    )
```
